256 devices in a mesh: row: 8 (over z), col: 32 (over x, y, core).
Axes of the slice: x: 4, y: 4, z: 8, core: 2. Of those that a mesh axis runs over, the one named last changes fastest.
Arguments:
- tokens: bfloat16 [1024, 8192], P('row', 'col'), may hold values from -6 to 6
- gate_weight: bfloat16 [8192, 16384], P('row', 'col'), may hold values from -0.125 to 0.125
- up_weight: bfloat16 [8192, 16384], P('row', 'col'), may hold values from -0.125 to 0.125
- gate_mask: int32 [128, 256], P('row', 'col'), may hold values from 0 to 1, as said below
- up_mask: int32 [128, 256], P('row', 'col'), may hold values from 0 to 1, as said below
- grad_hidden: bfloat16 [1024, 16384], P('row', 'col'), may hold values from -1.1953125 to 1.1953125
Outputs:
- hidden: bfloat16 [1024, 16384], P('row', 'col')
- grad_input: bfloat16 [1024, 8192], P(None, ('row', 'col'))
- grad_gate: bfloat16 [8192, 16384], P('row', 'col')
- grad_up: bfloat16 [8192, 16384], P('row', 'col')
The draws below stay inside these ranges and needn't reach their ends.
Inputs may be any that keep to these rules, and one draw needn't show every extreme that they name: `gate_mask`: 1 keeps a block of 64 x 64 weights, 0 drops it. `up_mask`: 1 keeps a block of 64 x 64 weights, 0 drops it.
All inputs are finite; a program needn't handle non-finite values.
Results may differ from the reference program's by a relative error of at most 0.024.
Values may be sent and summed in bfloat16 or wider, within the bound.
A program may use at most 128 MiB of HBM per device.

```python
import jax
import jax.numpy as jnp
from jax import lax

D = 8192
FF = 16384
BLOCK = 64
TOKENS = 1024
N_ROW = 8
N_COL = 32


def tiled_mask(key):
    key_levels, key_cells = jax.random.split(key)
    levels = jax.random.randint(key_levels, (N_ROW, N_COL), 1, 11)
    block_rows = D // BLOCK
    block_cols = FF // BLOCK
    spread = jnp.repeat(jnp.repeat(levels, block_rows // N_ROW, axis=0), block_cols // N_COL, axis=1)
    cells = jax.random.randint(key_cells, (block_rows, block_cols), 0, 20)
    return jnp.where(cells < spread, 1, 0).astype(jnp.int32)


def draw_gate_mask(key, part):
    key = jax.random.fold_in(key, 11)
    return tiled_mask(key)


def draw_up_mask(key, part):
    key = jax.random.fold_in(key, 12)
    return tiled_mask(key)


def steps_of(own_key, shape, cuts, least, high):
    gain = 1.0
    for position, shards_of in cuts:
        draws = jax.random.uniform(jax.random.fold_in(jax.random.fold_in(own_key, 6), position), (shards_of,), jnp.float32, least / len(cuts), high / len(cuts))
        gain = gain * jnp.repeat(jnp.exp(draws), shape[position] // shards_of).reshape((-1,) + (1,) * (len(shape) - 1 - position))
    return gain


def bell_draw(own_key, extent, scale, bound, cuts=(), held_as=jnp.bfloat16):
    array = scale * jax.random.normal(own_key, extent, jnp.float32)
    if cuts:
        array = array * steps_of(own_key, extent, cuts, -0.22, 0.18)
    return jnp.clip(array, -bound, bound).astype(held_as)


def setup_inputs(seed: int = 0) -> dict:
    keys = jax.random.split(jax.random.key(seed), 7)
    tokens = bell_draw(keys[0], (TOKENS, D), 1.0, 6.0, ((0, 8), (1, 32)))
    gate_weight = bell_draw(keys[1], (D, FF), (D // 4) ** -0.5, 0.125, ((0, 8), (1, 32)))
    up_weight = bell_draw(keys[2], (D, FF), (D // 4) ** -0.5, 0.125, ((0, 8), (1, 32)))
    gate_mask = draw_gate_mask(jax.random.fold_in(keys[6], 71), 0)
    up_mask = draw_up_mask(jax.random.fold_in(keys[6], 71), 0)
    grad_hidden = bell_draw(keys[5], (TOKENS, FF), 0.2, 1.1953125, ((0, 8), (1, 32)))
    return dict(tokens=tokens, gate_weight=gate_weight, up_weight=up_weight, gate_mask=gate_mask, up_mask=up_mask, grad_hidden=grad_hidden)


def expand(mask, block_size):
    rows, cols = mask.shape
    grid = jnp.broadcast_to(mask[:, None, :, None], (rows, block_size, cols, block_size))
    return grid.reshape(rows * block_size, cols * block_size)


def reference(tokens, gate_weight, up_weight, gate_mask, up_mask, grad_hidden):
    gate_keep = expand(gate_mask, BLOCK) > 0
    up_keep = expand(up_mask, BLOCK) > 0
    gate_masked = jnp.where(gate_keep, gate_weight, jnp.zeros_like(gate_weight))
    up_masked = jnp.where(up_keep, up_weight, jnp.zeros_like(up_weight))
    gate_value = jnp.dot(tokens, gate_masked, preferred_element_type=jnp.float32)
    up_value = jnp.dot(tokens, up_masked, preferred_element_type=jnp.float32)
    sigmoid_gate = jax.nn.sigmoid(gate_value)
    activated = gate_value * sigmoid_gate
    hidden = (activated * up_value).astype(jnp.bfloat16)
    upstream = grad_hidden.astype(jnp.float32)
    grad_gate_value = (upstream * up_value * sigmoid_gate * (1.0 + gate_value * (1.0 - sigmoid_gate))).astype(jnp.bfloat16)
    grad_up_value = (upstream * activated).astype(jnp.bfloat16)
    block_width = FF // N_COL
    contract = (((1,), (1,)), ((), ()))

    def add_block(index, total):
        start = (index * block_width).astype(jnp.int32)
        grad_g = lax.dynamic_slice_in_dim(grad_gate_value, start, block_width, 1)
        grad_u = lax.dynamic_slice_in_dim(grad_up_value, start, block_width, 1)
        weight_g = lax.dynamic_slice_in_dim(gate_masked, start, block_width, 1)
        weight_u = lax.dynamic_slice_in_dim(up_masked, start, block_width, 1)
        partial_sum = lax.dot_general(grad_g, weight_g, contract, preferred_element_type=jnp.float32)
        partial_sum = partial_sum + lax.dot_general(grad_u, weight_u, contract, preferred_element_type=jnp.float32)
        rounded = lax.optimization_barrier(partial_sum.astype(jnp.bfloat16)).astype(jnp.float32)
        return total + rounded

    start_total = jnp.zeros((tokens.shape[0], tokens.shape[1]), jnp.float32)
    grad_input = lax.fori_loop(0, N_COL, add_block, start_total).astype(jnp.bfloat16)
    over_tokens = (((0,), (0,)), ((), ()))
    gate_sums = lax.dot_general(tokens, grad_gate_value, over_tokens, preferred_element_type=jnp.float32)
    grad_gate = jnp.where(gate_keep, gate_sums, jnp.zeros_like(gate_sums)).astype(jnp.bfloat16)
    up_sums = lax.dot_general(tokens, grad_up_value, over_tokens, preferred_element_type=jnp.float32)
    grad_up = jnp.where(up_keep, up_sums, jnp.zeros_like(up_sums)).astype(jnp.bfloat16)
    return hidden, grad_input, grad_gate, grad_up
```

```python
import functools

import jax
import jax.numpy as jnp
from jax import lax
from jax.experimental import pallas as pl
from jax.experimental.pallas import tpu as pltpu
from jax.sharding import PartitionSpec as P

MESH = pl.DeviceIdType.MESH
BF16 = jnp.bfloat16
F32 = jnp.float32

NZ = 8
NS = 4
TB = 128
DB = 1024
SW = 256
QW = 256
OFFSET = (0, 1, -1, 2, -2, 3, -3, 4)
GROUPS = ((0, 1), (1, 2), (3, 2), (5, 2), (7, 1))


def slot_of(rel):
    high = rel // 5
    return (1 - high) * (2 * rel - 1) + high * (16 - 2 * rel) + 1 - (rel + 7) // 8


def remote(src, dst, send, recv, device):
    return pltpu.make_async_remote_copy(
        src_ref=src, dst_ref=dst, send_sem=send, recv_sem=recv, device_id=device, device_id_type=MESH
    )


def kernel(
    tokens, wg, wu, mg, mu, gh,
    hidden, git, og, ou,
    wgv, wuv, wp, we, mex, tv, tt, sb, rb, gv, ps, cr, sx, xr, sy, yr,
    lsem, osem, a1s, tr, aus, avs, afs, acs, bs, br, dsm, dr, ecs, ecr, exs, exr, eys, eyr,
):
    z = lax.axis_index("row")
    c = lax.axis_index("col")
    m = c // 2
    k = c % 2
    x, y = m // 4, m % 4
    u = x + k * (y - x)
    v = y + k * (x - y)
    q = c % 4
    plane = c // 4

    def dev(u_, v_):
        x_ = u_ + k * (v_ - u_)
        y_ = v_ + k * (u_ - v_)
        return (z, (x_ * 4 + y_) * 2 + k)

    def tpiece(slot, q_):
        return tv.at[slot, :, pl.ds(pl.multiple_of(q_ * QW, QW), QW)]

    def piece(u_, v_, k_):
        x_ = u_ + k_ * (v_ - u_)
        y_ = v_ + k_ * (u_ - v_)
        m_ = x_ * 4 + y_
        return slot_of((m_ // 2 + 16 - 2 * z) % NZ), 2 * (m_ % 2) + k_

    upd = ((z + 1) % NZ, c)
    down = ((z + NZ - 1) % NZ, c)
    ring = (upd, down)
    other = (z, c + 1 - 2 * k)
    to = (plane, 4 * ((z + plane) % NZ) + q)
    frm = ((plane + NZ - z) % NZ, 4 * z + q)
    self_piece = jnp.logical_and(z == 0, c < 4)

    barrier = pltpu.get_barrier_semaphore()
    for d in range(1, 4):
        for target in (dev((u + d) % 4, v), dev(u, (v + d) % 4)):
            pl.semaphore_signal(barrier, inc=1, device_id=target, device_id_type=MESH)
    for target in (other, upd, down):
        pl.semaphore_signal(barrier, inc=1, device_id=target, device_id_type=MESH)

    @pl.when(jnp.logical_not(self_piece))
    def _():
        pl.semaphore_signal(barrier, inc=1, device_id=frm, device_id_type=MESH)

    load_g = pltpu.make_async_copy(wg, wgv, lsem.at[0])
    load_u = pltpu.make_async_copy(wu, wuv, lsem.at[1])
    load_g.start()
    load_u.start()
    pl.semaphore_wait(barrier, 10 - (1 - (z + 7) // 8) * (1 - (c + 28) // 32))

    s0, q0 = piece(u, v, k)
    d0 = slot_of((z + NZ - plane) % NZ)
    send0 = remote(tokens, tpiece(d0, q), a1s.at[0], tr.at[d0 * 4 + q], to)
    own = remote(tokens, tpiece(s0, q0), a1s.at[0], tr.at[s0 * 4 + q0], to)

    @pl.when(jnp.logical_not(self_piece))
    def _():
        send0.start()

    @pl.when(self_piece)
    def _():
        local = pltpu.make_async_copy(tokens, tpiece(s0, q0), lsem.at[2])
        local.start()
        local.wait()

    lane = lax.broadcasted_iota(jnp.int32, (16, 128), 1) // 64
    for which, mask in enumerate((mg, mu)):
        kept = jnp.where(mask[...] > 0, 1.0, 0.0).astype(F32)
        for s in range(NS):
            kept_wide = jnp.where(lane == 0, kept[:, 2 * s : 2 * s + 1], kept[:, 2 * s + 1 : 2 * s + 2])
            for i in range(16):
                mex[i, :, s * SW + which * 128 : s * SW + which * 128 + 128] = jnp.broadcast_to(
                    kept_wide[i : i + 1], (8, 128)
                )
    load_g.wait()
    load_u.wait()

    @pl.loop(0, 16)
    def _(i):
        rows = pl.ds(pl.multiple_of(i * 64, 64), 64)
        flip = (i % 4) * 4 + i // 4
        for s in range(NS):
            for which, raw in enumerate((wgv, wuv)):
                cols = slice(s * SW + which * 128, s * SW + which * 128 + 128)
                val = raw[rows, s * 128 : s * 128 + 128].astype(F32).reshape(8, 8, 128)
                val = (val * mex[i, :, cols]).reshape(64, 128).astype(BF16)
                wp[rows, cols] = val
                we[0, pl.ds(pl.multiple_of(i * 32, 32), 32), cols] = val[:32]
                we[1, pl.ds(pl.multiple_of(flip * 32, 32), 32), cols] = val[32:]

    def send_piece(su, qu, sem, target):
        remote(tpiece(su, qu), tpiece(su, qu), sem, tr.at[su * 4 + qu], target).start()

    def wait_piece(su, qu):
        remote(tpiece(su, qu), tpiece(su, qu), a1s.at[0], tr.at[su * 4 + qu], other).wait_recv()

    vright, vleft = dev(u, (v + 1) % 4), dev(u, (v + 3) % 4)

    @pl.when(jnp.logical_not(self_piece))
    def _():
        own.wait_recv()

    for d in range(4):
        su, qu = piece((u + d) % 4, v, k)
        if d == 0:
            for e in range(1, 4):
                send_piece(su, qu, aus.at[e - 1], dev((u + e) % 4, v))
        else:
            wait_piece(su, qu)
        send_piece(su, qu, avs.at[0, d], vright)
        send_piece(su, qu, avs.at[1, d], vleft)
        send_piece(su, qu, acs.at[d], other)
    for d in range(4):
        for side, vv, onward in ((0, (v + 3) % 4, vright), (1, (v + 1) % 4, vleft)):
            su, qu = piece((u + d) % 4, vv, k)
            wait_piece(su, qu)
            if (d < 2) == (side == 0):
                send_piece(su, qu, afs.at[d], onward)
            send_piece(su, qu, acs.at[4 + 2 * d + side], other)
    for d in range(4):
        su, qu = piece((u + d) % 4, (v + 2) % 4, k)
        wait_piece(su, qu)
        send_piece(su, qu, acs.at[12 + d], other)
    for d in range(4):
        for e in range(4):
            su, qu = piece(d, e, 1 - k)
            wait_piece(su, qu)

    def transposed(slot, s):
        cols = slice(s * QW, s * QW + QW)
        tt[cols, slot * TB : slot * TB + TB] = tv[slot, :, cols].T

    def scols(s):
        return pl.ds(pl.multiple_of(s * SW, SW), SW)

    def b_copy(d, step, s):
        return remote(sb.at[d, step, s], rb.at[d, step, s], bs.at[d, step, s], br.at[d, step, s], ring[d])

    def partial_sum(slot, count, s):
        rows = tv[slot : slot + count].reshape(count * TB, DB)
        return jnp.dot(rows, wp[:, s * SW : s * SW + SW], preferred_element_type=F32)

    for s in range(NS):
        d = s // 2
        sb[d, 0, s] = partial_sum(7, 1, s).astype(BF16)
        b_copy(d, 0, s).start()
    for step, slot in ((1, 5), (2, 3), (3, 1)):
        for s in range(NS):
            val = partial_sum(slot, 2, s)
            for d in range(2):
                term = val[d * TB : d * TB + TB]
                if step > 1 or s // 2 == d:
                    b_copy(d, step - 1, s).wait_recv()
                    term = term + rb[d, step - 1, s].astype(F32)
                sb[d, step, s] = term.astype(BF16)
                b_copy(d, step, s).start()
            transposed(slot, s)
            transposed(slot + 1, s)

    def d_copy(dst, src, s, d, step):
        cols = slice(s * SW, s * SW + SW)
        return remote(gv.at[src, :, cols], gv.at[dst, :, cols], dsm.at[d, step, s], dr.at[dst, s], ring[d])

    def d_wait(slot, s):
        cols = slice(s * SW, s * SW + SW)
        part = gv.at[slot, :, cols]
        remote(part, part, dsm.at[0, 0, 0], dr.at[slot, s], upd).wait_recv()

    for s in range(NS):
        val = partial_sum(0, 1, s)
        for d in range(2):
            b_copy(d, 3, s).wait_recv()
            val = val + rb[d, 3, s].astype(F32)
        gate, up = val[:, :128], val[:, 128:]
        hcols = slice(s * 128, s * 128 + 128)
        up_grad = gh[:, hcols].astype(F32)
        sig = 1.0 / (1.0 + jnp.exp(-gate))
        act = gate * sig
        hidden[:, hcols] = (act * up).astype(BF16)
        gv[0, :, s * SW : s * SW + 128] = (up_grad * up * sig * (1.0 + gate * (1.0 - sig))).astype(BF16)
        gv[0, :, s * SW + 128 : s * SW + SW] = (up_grad * act).astype(BF16)
        d_copy(2, 0, s, 0, 0).start()
        d_copy(1, 0, s, 1, 0).start()
        transposed(0, s)
        transposed(7, s)

    def grads_of(g):
        first, count = GROUPS[g]
        return gv[first : first + count].reshape(count * TB, DB)

    def half_dot(g, side, i):
        rows = we[side, i * 256 : i * 256 + 256, :]
        out = lax.dot_general(rows, grads_of(g), (((1,), (1,)), ((), ())), preferred_element_type=F32)
        return out.reshape(2, 4, 32, GROUPS[g][1] * TB)

    def wide(ref, g, *index):
        w = GROUPS[g][1] * TB
        rest = len(ref.shape) - 1 - len(index) - 1
        return ref.at[(g,) + index + (slice(None),) * rest + (slice(0, w),)]

    def core_copy(g):
        return remote(wide(ps, g), wide(cr, g), ecs.at[g], ecr.at[g], other)

    def x_copy(g, d):
        return remote(
            wide(sx, g, (u + d) % 4), wide(xr, g, d - 1), exs.at[g, d - 1], exr.at[g, d - 1], dev((u + d) % 4, v)
        )

    def y_copy(g, d):
        return remote(
            wide(sy, g, (v + d) % 4), wide(yr, g, d - 1), eys.at[g, d - 1], eyr.at[g, d - 1], dev(u, (v + d) % 4)
        )

    def e1(g):
        for i in range(2):
            wide(ps, g)[2 * i : 2 * i + 2] = half_dot(g, 1 - k, i).astype(BF16)
        core_copy(g).start()

    def e2(g):
        for i in range(2):
            val = half_dot(g, k, i)
            if i == 0:
                core_copy(g).wait_recv()
            val = val + wide(cr, g)[2 * i : 2 * i + 2].astype(F32)
            wide(sx, g)[2 * i : 2 * i + 2] = val.astype(BF16)
        for d in range(1, 4):
            x_copy(g, d).start()

    def e3(g):
        val = wide(sx, g, u)[...].astype(F32)
        for d in range(1, 4):
            x_copy(g, d).wait_recv()
            val = val + wide(xr, g, d - 1)[...].astype(F32)
        wide(sy, g)[...] = val.astype(BF16)
        for d in range(1, 4):
            y_copy(g, d).start()

    def e4(g):
        first, count = GROUPS[g]
        val = wide(sy, g, v)[...].astype(F32)
        for d in range(1, 4):
            y_copy(g, d).wait_recv()
            val = val + wide(yr, g, d - 1)[...].astype(F32)
        val = val.astype(BF16)
        for j in range(count):
            block = (z + NZ + OFFSET[first + j]) % NZ
            git[:, pl.ds(pl.multiple_of(block * TB, TB), TB)] = val[:, j * TB : j * TB + TB]

    e1(0)
    for step in range(1, 5):
        for s in range(NS):
            if step < 4:
                for d, slot in ((0, 2 * step), (1, 2 * step - 1)):
                    d_wait(slot, s)
                    if step < 3 or s // 2 == d:
                        d_copy(min(slot + 2, 7), slot, s, d, step).start()
            else:
                d_wait(7, s)
            g = step - 1
            if s == 0:
                e2(g)
            elif s == 1 and g > 0:
                e4(g - 1)
            elif s == 2:
                e3(g)
        e1(step)

    def weight_rows(i):
        rows = slice(i * 256, i * 256 + 256)
        for s in range(NS):
            right = gv[:, :, s * SW : s * SW + SW].reshape(NZ * TB, SW)
            val = jnp.dot(tt[rows, :], right, preferred_element_type=F32)
            for b in range(4):
                row = i * 4 + b
                for which, out in enumerate((og, ou)):
                    cols = slice(s * SW + which * 128, s * SW + which * 128 + 128)
                    keep = mex[row, 0:1, cols] > 0.0
                    part = val[b * 64 : b * 64 + 64, which * 128 : which * 128 + 128]
                    out[row * 64 : row * 64 + 64, s * 128 : s * 128 + 128] = jnp.where(keep, part, 0.0).astype(BF16)

    e4(3)
    e2(4)
    weight_rows(0)
    e3(4)
    weight_rows(1)
    e4(4)
    weight_rows(2)
    weight_rows(3)

    @pl.when(jnp.logical_not(self_piece))
    def _():
        send0.wait_send()

    def sent(sem):
        remote(tpiece(0, 0), tpiece(0, 0), sem, tr.at[0], other).wait_send()

    for d in range(3):
        sent(aus.at[d])
    for d in range(4):
        sent(avs.at[0, d])
        sent(avs.at[1, d])
        sent(afs.at[d])
    for d in range(16):
        sent(acs.at[d])
    for d in range(2):
        for s in range(NS):
            if s // 2 == d:
                b_copy(d, 0, s).wait_send()
            for step in range(1, 4):
                b_copy(d, step, s).wait_send()
            for step in range(4):
                if step < 3 or s // 2 == d:
                    d_copy(1, 0, s, d, step).wait_send()
    for g in range(len(GROUPS)):
        core_copy(g).wait_send()
        for d in range(1, 4):
            x_copy(g, d).wait_send()
            y_copy(g, d).wait_send()


def shards(tokens, gate_weight, up_weight, gate_mask, up_mask, grad_hidden):
    vmem = pl.BlockSpec(memory_space=pltpu.VMEM)
    hbm = pl.BlockSpec(memory_space=pl.ANY)
    dma = pltpu.SemaphoreType.DMA
    ng = len(GROUPS)
    hidden, git, og, ou = pl.pallas_call(
        kernel,
        out_shape=(
            jax.ShapeDtypeStruct((TB, 512), BF16),
            jax.ShapeDtypeStruct((32, NZ * TB), BF16),
            jax.ShapeDtypeStruct((DB, 512), BF16),
            jax.ShapeDtypeStruct((DB, 512), BF16),
        ),
        in_specs=[hbm, hbm, hbm, vmem, vmem, vmem],
        out_specs=(vmem, vmem, vmem, vmem),
        scratch_shapes=[
            pltpu.VMEM((DB, 512), BF16),
            pltpu.VMEM((DB, 512), BF16),
            pltpu.VMEM((DB, DB), BF16),
            pltpu.VMEM((2, 512, DB), BF16),
            pltpu.VMEM((16, 8, DB), F32),
            pltpu.VMEM((NZ, TB, DB), BF16),
            pltpu.VMEM((DB, NZ * TB), BF16),
            pltpu.VMEM((2, 4, NS, TB, SW), BF16),
            pltpu.VMEM((2, 4, NS, TB, SW), BF16),
            pltpu.VMEM((NZ, TB, DB), BF16),
            pltpu.VMEM((ng, 4, 4, 32, 256), BF16),
            pltpu.VMEM((ng, 4, 4, 32, 256), BF16),
            pltpu.VMEM((ng, 4, 4, 32, 256), BF16),
            pltpu.VMEM((ng, 3, 4, 32, 256), BF16),
            pltpu.VMEM((ng, 4, 32, 256), BF16),
            pltpu.VMEM((ng, 3, 32, 256), BF16),
            dma((3,)),
            dma((2,)),
            dma((1,)),
            dma((32,)),
            dma((3,)),
            dma((2, 4)),
            dma((4,)),
            dma((16,)),
            dma((2, 4, NS)),
            dma((2, 4, NS)),
            dma((2, 4, NS)),
            dma((NZ, NS)),
            dma((ng,)),
            dma((ng,)),
            dma((ng, 3)),
            dma((ng, 3)),
            dma((ng, 3)),
            dma((ng, 3)),
        ],
        compiler_params=pltpu.CompilerParams(
            collective_id=0, has_side_effects=True, vmem_limit_bytes=48 * 1024 * 1024
        ),
    )(tokens, gate_weight, up_weight, gate_mask, up_mask, grad_hidden)
    return hidden, git.T, og, ou


def solution(mesh):
    return jax.shard_map(
        shards,
        mesh=mesh,
        in_specs=(P("row", "col"),) * 6,
        out_specs=(P("row", "col"), P(None, ("row", "col")), P("row", "col"), P("row", "col")),
        check_vma=False,
    )
```

```python
import jax
import jax.numpy as jnp
from jax import lax
from jax.experimental import pallas as pl
from jax.experimental.pallas import tpu as pltpu
from jax.sharding import PartitionSpec as P

MESH = pl.DeviceIdType.MESH
BF16 = jnp.bfloat16
F32 = jnp.float32

NZ = 8
NS = 4
TB = 128
DB = 1024
SW = 256
QW = 256
OFFSET = (0, 1, -1, 2, -2, 3, -3, 4)
GROUPS = ((0, 1), (1, 2), (3, 2), (5, 2), (7, 1))
PLACE = ((2, 1), (1, 1), (3, 1), (2, 0), (0, 1), (1, 0), (3, 0), (0, 0))
SLOT_AT = tuple(PLACE.index((i % 4, i // 4)) for i in range(8))
REL = tuple(o % NZ for o in OFFSET)
SLOT_OF = tuple(REL.index(r) for r in range(NZ))


def pick(table, i):
    return sum(t * (1 - ((i - j) * (i - j) + 63) // 64) for j, t in enumerate(table))


def remote(src, dst, send, recv, device):
    return pltpu.make_async_remote_copy(
        src_ref=src, dst_ref=dst, send_sem=send, recv_sem=recv, device_id=device, device_id_type=MESH
    )


def kernel(
    tokens, wg, wu, mg, mu, gh,
    hidden_out, git_out, og_out, ou_out,
    wgv, wuv, ghv, hidden, git, og, ou, wp, we, mex, tv, tt, sb, rb, gv,
    ps1, ps2, cr1, cr2, sx1, sx2, er1, er2,
    lsem, osem, ts, tr, bs, br, dsm, dr, ecs, ecr, exs, exr,
):
    z = lax.axis_index("row")
    c = lax.axis_index("col")
    m = c // 2
    k = c % 2
    x, y = m // 4, m % 4
    u = x + k * (y - x)
    v = y + k * (x - y)
    x0, y0 = z // 2, 2 * (z % 2)
    u0 = x0 + k * (y0 - x0)

    def dev(u_, v_):
        x_ = u_ + k * (v_ - u_)
        y_ = v_ + k * (u_ - v_)
        return (z, (x_ * 4 + y_) * 2 + k)

    def tpiece(slot, q_):
        return tv.at[slot, :, pl.ds(pl.multiple_of(q_ * QW, QW), QW)]

    def piece(u_, v_):
        dx = (u_ + k * (v_ - u_) + 4 - x0) % 4
        dy = (v_ + k * (u_ - v_) + 4 - y0) % 4
        return pick(SLOT_AT, dx + 4 * (dy // 2)), 2 * (dy % 2) + k

    upd = ((z + 1) % NZ, c)
    down = ((z + NZ - 1) % NZ, c)
    ring = (upd, down)
    other = (z, c + 1 - 2 * k)

    plane = c // 4
    slot_there = pick(SLOT_OF, (z + NZ - plane) % NZ)
    to_x = (plane // 2 + pick([p[0] for p in PLACE], slot_there)) % 4
    to_y = (2 * (plane % 2) + 2 * pick([p[1] for p in PLACE], slot_there) + m % 2) % 4
    to = (plane, (to_x * 4 + to_y) * 2 + k)
    s0, q0 = piece(u, v)
    frm = ((z + pick(REL, s0)) % NZ, 4 * z + q0)

    load_g = pltpu.make_async_copy(wg, wgv, lsem.at[0])
    load_u = pltpu.make_async_copy(wu, wuv, lsem.at[1])
    load_h = pltpu.make_async_copy(gh, ghv, lsem.at[2])
    load_g.start()
    load_u.start()
    load_h.start()

    barrier = pltpu.get_barrier_semaphore()
    near = [(z, (((x + d // 4) % 4) * 4 + (y + d % 4) % 4) * 2 + k) for d in range(16)]
    for target in near[1:] + [other, upd, down, frm]:
        pl.semaphore_signal(barrier, inc=1, device_id=target, device_id_type=MESH)
    pl.semaphore_wait(barrier, 19)

    remote(tokens, tpiece(slot_there, c % 4), ts.at[0], tr.at[slot_there * 4 + c % 4], to).start()

    lane = lax.broadcasted_iota(jnp.int32, (16, 128), 1) // 64
    for which, mask in enumerate((mg, mu)):
        kept = jnp.where(mask[...] > 0, 1.0, 0.0).astype(F32).T
        for s in range(NS):
            kept_wide = jnp.where(lane == 0, kept[:, 2 * s : 2 * s + 1], kept[:, 2 * s + 1 : 2 * s + 2])
            for i in range(16):
                mex[i, :, s * SW + which * 128 : s * SW + which * 128 + 128] = jnp.broadcast_to(
                    kept_wide[i : i + 1], (8, 128)
                )
    load_g.wait()
    load_u.wait()
    load_h.wait()

    @pl.loop(0, 16)
    def _(i):
        rows = pl.ds(pl.multiple_of(i * 64, 64), 64)
        half = pl.ds(pl.multiple_of(i * 32, 32), 32)
        for s in range(NS):
            for which, raw in enumerate((wgv, wuv)):
                cols = slice(s * SW + which * 128, s * SW + which * 128 + 128)
                val = raw[rows, s * 128 : s * 128 + 128].astype(F32).reshape(8, 8, 128)
                val = (val * mex[i, :, cols]).reshape(64, 128).astype(BF16)
                wp[rows, cols] = val
                we[0, half, cols] = val[:32]
                we[1, half, cols] = val[32:]

    def send_piece(su, qu, target):
        remote(tpiece(su, qu), tpiece(su, qu), ts.at[0], tr.at[su * 4 + qu], target).start()

    def wait_piece(su, qu):
        remote(tpiece(su, qu), tpiece(su, qu), ts.at[0], tr.at[su * 4 + qu], other).wait_recv()

    wait_piece(s0, q0)
    for d in (1, 3, 2):
        send_piece(s0, q0, dev((u + d) % 4, v))
    for d in (1, 3, 2):
        send_piece(s0, q0, dev(u, (v + d) % 4))
    for off in (0, 1, 3, 2):
        line = (u0 + off) % 4

        @pl.when(line != u)
        def _(line=line):
            su, qu = piece(line, v)
            wait_piece(su, qu)
            for d in (1, 3, 2):
                send_piece(su, qu, dev(u, (v + d) % 4))

    def swap(slot):
        for b in range(2):
            x_ = (x0 + PLACE[slot][0]) % 4
            y_ = (y0 + 2 * PLACE[slot][1] + b) % 4
            q_ = 2 * b + k

            @pl.when(y_ + k * (x_ - y_) != v)
            def _(q_=q_):
                wait_piece(slot, q_)

            send_piece(slot, q_, other)

    def ready(slot):
        for b in range(2):
            wait_piece(slot, 2 * b + 1 - k)

    def transposed(slot, s):
        cols = slice(s * QW, s * QW + QW)
        tt[cols, slot * TB : slot * TB + TB] = tv[slot, :, cols].T

    def b_copy(d, step, s):
        i = s % 2 if step == 0 else 4 * step - 2 + s
        return remote(sb.at[d, i], rb.at[d, i], bs.at[d], br.at[d, i], ring[d])

    def b_in(d, step, s):
        b_copy(d, step, s).wait_recv()
        return rb[d, s % 2 if step == 0 else 4 * step - 2 + s].astype(F32)

    def b_out(d, step, s, val):
        sb[d, s % 2 if step == 0 else 4 * step - 2 + s] = val.astype(BF16)
        b_copy(d, step, s).start()

    def partial_sum(slot, count, s):
        rows = tv[slot : slot + count].reshape(count * TB, DB)
        return jnp.dot(rows, wp[:, s * SW : s * SW + SW], preferred_element_type=F32)

    for slot in (7, 5, 6):
        swap(slot)
    ready(7)
    for s in (0, 2, 1, 3):
        b_out(s // 2, 0, s, partial_sum(7, 1, s))
    for slot in (3, 4):
        swap(slot)
    ready(5)
    ready(6)
    for d, s in ((0, 2), (1, 0), (0, 3), (1, 1)):
        b_out(d, 1, s, partial_sum(5 + d, 1, s))
    for slot in (1, 2, 0):
        swap(slot)
    for s in range(NS):
        transposed(7, s)
    for d, s in ((0, 0), (1, 2), (0, 1), (1, 3)):
        val = partial_sum(5 + d, 1, s)
        b_out(d, 1, s, val + b_in(d, 0, s))
    for step, slot in ((2, 3), (3, 1)):
        ready(slot)
        ready(slot + 1)
        for s in range(NS):
            val = partial_sum(slot, 2, s)
            for d in range(2):
                b_out(d, step, s, val[d * TB : d * TB + TB] + b_in(d, step - 1, s))
            transposed(slot, s)
            transposed(slot + 1, s)
            transposed(slot + 2, s)
            if step == 2:
                transposed(6, s)
    ready(0)

    def d_copy(dst, src, s, d):
        cols = slice(s * SW, s * SW + SW)
        return remote(gv.at[src, :, cols], gv.at[dst, :, cols], dsm.at[d], dr.at[dst, s], ring[d])

    def d_wait(slot, s):
        d_copy(slot, slot, s, 0).wait_recv()

    for s in range(NS):
        val = partial_sum(0, 1, s)
        for d in range(2):
            val = val + b_in(d, 3, s)
        gate, up = val[:, :128], val[:, 128:]
        hcols = slice(s * 128, s * 128 + 128)
        up_grad = ghv[:, hcols].astype(F32)
        sig = 1.0 / (1.0 + jnp.exp(-gate))
        act = gate * sig
        gv[0, :, s * SW : s * SW + 128] = (up_grad * up * sig * (1.0 + gate * (1.0 - sig))).astype(BF16)
        gv[0, :, s * SW + 128 : s * SW + SW] = (up_grad * act).astype(BF16)
        d_copy(2, 0, s, 0).start()
        d_copy(1, 0, s, 1).start()
        hidden[:, hcols] = (act * up).astype(BF16)
        transposed(0, s)
    store_h = pltpu.make_async_copy(hidden, hidden_out, osem.at[0])
    store_h.start()

    def of_group(one, two, g):
        return one.at[g // 4] if GROUPS[g][1] == 1 else two.at[g - 1]

    def core_dot(g, side):
        first, count = GROUPS[g]
        grads = gv[first : first + count].reshape(count * TB, DB)
        out = lax.dot_general(we[side], grads, (((1,), (1,)), ((), ())), preferred_element_type=F32)
        return out.reshape(16, 32, count * TB)

    def core_copy(g):
        return remote(of_group(ps1, ps2, g), of_group(cr1, cr2, g), ecs.at[g], ecr.at[g], other)

    def e1(g):
        of_group(ps1, ps2, g)[...] = core_dot(g, 1 - k).astype(BF16)
        core_copy(g).start()

    def e2(g):
        val = core_dot(g, k)
        core_copy(g).wait_recv()
        sums = of_group(sx1, sx2, g)
        sums[...] = (val + of_group(cr1, cr2, g)[...].astype(F32)).astype(BF16)
        for d in range(1, 16):
            chip = ((x + d // 4) % 4) * 4 + (y + d % 4) % 4
            remote(sums.at[chip], of_group(er1, er2, g).at[d - 1], exs.at[g], exr.at[g], near[d]).start()

    def plane_all(g):
        sums, got = of_group(sx1, sx2, g), of_group(er1, er2, g)
        return remote(sums.at[0:15], got, exs.at[g], exr.at[g], other)

    def e3(g):
        first, count = GROUPS[g]
        plane_all(g).wait_recv()
        val = of_group(sx1, sx2, g)[m].astype(F32)
        for d in range(15):
            val = val + of_group(er1, er2, g)[d].astype(F32)
        val = val.astype(BF16)
        for j in range(count):
            block = (z + NZ + OFFSET[first + j]) % NZ
            git[:, pl.ds(pl.multiple_of(block * TB, TB), TB)] = val[:, j * TB : j * TB + TB]

    for step in range(1, 4):
        for s in range(NS):
            for d, slot in ((0, 2 * step), (1, 2 * step - 1)):
                d_wait(slot, s)
                if step < 3 or s // 2 == d:
                    d_copy(min(slot + 2, 7), slot, s, d).start()
            if s == 0:
                e1(step - 1)
            elif s == 2:
                e2(step - 1)
            elif s == 3 and step > 1:
                e3(step - 2)
    d_wait(7, 0)
    d_wait(7, 2)
    e1(3)
    d_wait(7, 1)
    d_wait(7, 3)
    e1(4)
    e2(3)
    e2(4)

    def store_rows(i):
        rows = slice(i * 256, i * 256 + 256)
        return [
            pltpu.make_async_copy(val.at[rows], out.at[rows], osem.at[2 + 2 * i + j])
            for j, (val, out) in enumerate(((og, og_out), (ou, ou_out)))
        ]

    def weight_rows(i):
        rows = slice(i * 256, i * 256 + 256)
        for s in range(NS):
            right = gv[:, :, s * SW : s * SW + SW].reshape(NZ * TB, SW)
            val = jnp.dot(tt[rows, :], right, preferred_element_type=F32)
            for b in range(4):
                row = i * 4 + b
                for which, out in enumerate((og, ou)):
                    cols = slice(s * SW + which * 128, s * SW + which * 128 + 128)
                    keep = mex[row, 0:1, cols] > 0.0
                    part = val[b * 64 : b * 64 + 64, which * 128 : which * 128 + 128]
                    out[row * 64 : row * 64 + 64, s * 128 : s * 128 + 128] = jnp.where(keep, part, 0.0).astype(BF16)
        for copy in store_rows(i):
            copy.start()

    for i in range(4):
        weight_rows(i)
    e3(2)
    e3(3)
    e3(4)
    store_i = pltpu.make_async_copy(git, git_out, osem.at[1])
    store_i.start()

    remote(tv, tv, ts.at[0], tr.at[0], other).wait_send()
    for d in range(2):
        remote(sb.at[d], sb.at[d], bs.at[d], br.at[0, 0], other).wait_send()
        remote(sb.at[d], sb.at[d], dsm.at[d], br.at[0, 0], other).wait_send()
    for g in range(len(GROUPS)):
        core_copy(g).wait_send()
        plane_all(g).wait_send()
    store_h.wait()
    for i in range(4):
        for copy in store_rows(i):
            copy.wait()
    store_i.wait()


def finish(*refs):
    srcs, outs, held, sem = refs[:4], refs[4:8], refs[8:12], refs[12]
    parts = [(i, slice(j, j + 512)) for i in range(2, 4) for j in (0, 512)] + [(0, slice(0, TB)), (1, slice(0, 32))]
    loads = [pltpu.make_async_copy(srcs[i].at[r], held[i].at[r], sem.at[0, n]) for n, (i, r) in enumerate(parts)]
    stores = [pltpu.make_async_copy(held[i].at[r], outs[i].at[r], sem.at[1, n]) for n, (i, r) in enumerate(parts)]
    for load in loads:
        load.start()
    for load, store in zip(loads, stores):
        load.wait()
        store.start()
    for store in stores:
        store.wait()


def shards(tokens, gate_weight, up_weight, gate_mask, up_mask, grad_hidden):
    vmem = pl.BlockSpec(memory_space=pltpu.VMEM)
    hbm = pl.BlockSpec(memory_space=pl.ANY)
    dma = pltpu.SemaphoreType.DMA
    ng = len(GROUPS)
    shapes = (
        jax.ShapeDtypeStruct((TB, 512), BF16),
        jax.ShapeDtypeStruct((32, NZ * TB), BF16),
        jax.ShapeDtypeStruct((DB, 512), BF16),
        jax.ShapeDtypeStruct((DB, 512), BF16),
    )
    results = pl.pallas_call(
        kernel,
        out_shape=shapes,
        in_specs=[hbm, hbm, hbm, vmem, vmem, hbm],
        out_specs=(hbm,) * 4,
        scratch_shapes=[
            pltpu.VMEM((DB, 512), BF16),
            pltpu.VMEM((DB, 512), BF16),
            pltpu.VMEM((TB, 512), BF16),
            pltpu.VMEM((TB, 512), BF16),
            pltpu.VMEM((32, NZ * TB), BF16),
            pltpu.VMEM((DB, 512), BF16),
            pltpu.VMEM((DB, 512), BF16),
            pltpu.VMEM((DB, DB), BF16),
            pltpu.VMEM((2, 512, DB), BF16),
            pltpu.VMEM((16, 8, DB), F32),
            pltpu.VMEM((NZ, TB, DB), BF16),
            pltpu.VMEM((DB, NZ * TB), BF16),
            pltpu.VMEM((2, 14, TB, SW), BF16),
            pltpu.VMEM((2, 14, TB, SW), BF16),
            pltpu.VMEM((NZ, TB, DB), BF16),
            pltpu.VMEM((2, 16, 32, TB), BF16),
            pltpu.VMEM((3, 16, 32, 2 * TB), BF16),
            pltpu.VMEM((2, 16, 32, TB), BF16),
            pltpu.VMEM((3, 16, 32, 2 * TB), BF16),
            pltpu.VMEM((2, 16, 32, TB), BF16),
            pltpu.VMEM((3, 16, 32, 2 * TB), BF16),
            pltpu.VMEM((2, 15, 32, TB), BF16),
            pltpu.VMEM((3, 15, 32, 2 * TB), BF16),
            dma((3,)),
            dma((10,)),
            dma((1,)),
            dma((32,)),
            dma((2,)),
            dma((2, 14)),
            dma((2,)),
            dma((NZ, NS)),
            dma((ng,)),
            dma((ng,)),
            dma((ng,)),
            dma((ng,)),
        ],
        compiler_params=pltpu.CompilerParams(
            collective_id=0, has_side_effects=True, vmem_limit_bytes=56 * 1024 * 1024
        ),
    )(tokens, gate_weight, up_weight, gate_mask.T, up_mask.T, grad_hidden)
    hidden, git, og, ou = pl.pallas_call(
        finish,
        out_shape=shapes,
        in_specs=[hbm] * 4,
        out_specs=(hbm,) * 4,
        scratch_shapes=[pltpu.VMEM(shape.shape, BF16) for shape in shapes] + [dma((2, 6))],
        compiler_params=pltpu.CompilerParams(vmem_limit_bytes=56 * 1024 * 1024),
    )(*results)
    return hidden, git.T, og, ou


def solution(mesh):
    return jax.shard_map(
        shards,
        mesh=mesh,
        in_specs=(P("row", "col"),) * 6,
        out_specs=(P("row", "col"), P(None, ("row", "col")), P("row", "col"), P("row", "col")),
        check_vma=False,
    )
```

```python
import jax
import jax.numpy as jnp
from jax import lax
from jax.experimental import pallas as pl
from jax.experimental.pallas import tpu as pltpu
from jax.sharding import PartitionSpec as P

MESH = pl.DeviceIdType.MESH
BF16 = jnp.bfloat16
F32 = jnp.float32

NZ = 8
NS = 4
TB = 128
DB = 1024
SW = 256
QW = 256
HB = 64
HALVES = (slice(0, HB), slice(HB, TB))
OFFSET = (0, 1, -1, 2, -2, 3, -3, 4)
GROUPS = ((0, 1), (1, 2), (3, 2), (5, 2), (7, 1))
PLACE = ((2, 0), (1, 1), (2, 1), (0, 0), (3, 1), (3, 0), (0, 1), (1, 0))
SLOT_AT = tuple(PLACE.index((i % 4, i // 4)) for i in range(8))
REL = tuple(o % NZ for o in OFFSET)
EARLY = (0, 0, 0, 0, 0, 1, 1, 1)
SLOT_OF = tuple(REL.index(r) for r in range(NZ))


def pick(table, i):
    return sum(t * (1 - ((i - j) * (i - j) + 63) // 64) for j, t in enumerate(table))


def remote(src, dst, send, recv, device):
    return pltpu.make_async_remote_copy(
        src_ref=src, dst_ref=dst, send_sem=send, recv_sem=recv, device_id=device, device_id_type=MESH
    )


def kernel(
    tokens, wg, wu, mg, mu, gh,
    hidden_out, git_out, og_out, ou_out,
    mgv, muv, wgv, wuv, ghv, hidden, git, og, ou, wp, we, mex, tv, tt, sb, rb, gv,
    ps1, ps2, cr1, cr2, ow1, ow2, sx1, sx2, er1, er2,
    lsem, osem, ts, tr, bs, br, dsm, dr, ecs, ecr, exs, exr,
):
    z = lax.axis_index("row")
    c = lax.axis_index("col")
    m = c // 2
    k = c % 2
    x, y = m // 4, m % 4
    u = x + k * (y - x)
    v = y + k * (x - y)
    x0, y0 = z // 2, 2 * (z % 2)
    u0 = x0 + k * (y0 - x0)

    def dev(u_, v_):
        x_ = u_ + k * (v_ - u_)
        y_ = v_ + k * (u_ - v_)
        return (z, (x_ * 4 + y_) * 2 + k)

    def tpiece(slot, q_, h):
        return tv.at[slot, HALVES[h], pl.ds(pl.multiple_of(q_ * QW, QW), QW)]

    def piece(u_, v_):
        dx = (u_ + k * (v_ - u_) + 4 - x0) % 4
        dy = (v_ + k * (u_ - v_) + 4 - y0) % 4
        return pick(SLOT_AT, dx + 4 * (dy // 2)), 2 * (dy % 2) + k

    upd = ((z + 1) % NZ, c)
    down = ((z + NZ - 1) % NZ, c)
    ring = (upd, down)
    other = (z, c + 1 - 2 * k)

    plane = c // 4
    slot_there = pick(SLOT_OF, (z + NZ - plane) % NZ)
    to_x = (plane // 2 + pick([p[0] for p in PLACE], slot_there)) % 4
    to_y = (2 * (plane % 2) + 2 * pick([p[1] for p in PLACE], slot_there) + m % 2) % 4
    to = (plane, (to_x * 4 + to_y) * 2 + k)
    s0, q0 = piece(u, v)
    frm = ((z + pick(REL, s0)) % NZ, 4 * z + q0)

    load_mg = pltpu.make_async_copy(mg, mgv, lsem.at[3])
    load_mu = pltpu.make_async_copy(mu, muv, lsem.at[4])
    load_mg.start()
    load_mu.start()
    load_g = pltpu.make_async_copy(wg, wgv, lsem.at[0])
    load_u = pltpu.make_async_copy(wu, wuv, lsem.at[1])
    load_h = pltpu.make_async_copy(gh, ghv, lsem.at[2])
    load_g.start()
    load_u.start()
    load_h.start()

    barrier = pltpu.get_barrier_semaphore()
    near = [(z, (((x + d // 4) % 4) * 4 + (y + d % 4) % 4) * 2 + k) for d in range(16)]
    for target in near[1:] + [other, upd, down, frm]:
        pl.semaphore_signal(barrier, inc=1, device_id=target, device_id_type=MESH)
    pl.semaphore_wait(barrier, 19)

    for h in range(2):
        remote(
            tokens.at[HALVES[h]], tpiece(slot_there, c % 4, h), ts.at[0], tr.at[slot_there * 4 + c % 4, h], to
        ).start()

    lane = lax.broadcasted_iota(jnp.int32, (16, 128), 1) // 64
    load_mg.wait()
    load_mu.wait()
    for which, mask in enumerate((mgv, muv)):
        kept = jnp.where(mask[...] > 0, 1.0, 0.0).astype(F32).T
        for s in range(NS):
            kept_wide = jnp.where(lane == 0, kept[:, 2 * s : 2 * s + 1], kept[:, 2 * s + 1 : 2 * s + 2])
            for i in range(16):
                mex[i, :, s * SW + which * 128 : s * SW + which * 128 + 128] = jnp.broadcast_to(
                    kept_wide[i : i + 1], (8, 128)
                )
    load_g.wait()
    load_u.wait()
    load_h.wait()

    @pl.loop(0, 16)
    def _(i):
        rows = pl.ds(pl.multiple_of(i * 64, 64), 64)
        half = pl.ds(pl.multiple_of(i * 32, 32), 32)
        for s in range(NS):
            for which, raw in enumerate((wgv, wuv)):
                cols = slice(s * SW + which * 128, s * SW + which * 128 + 128)
                val = raw[rows, s * 128 : s * 128 + 128].astype(F32).reshape(8, 8, 128)
                val = (val * mex[i, :, cols]).reshape(64, 128).astype(BF16)
                wp[rows, cols] = val
                we[0, half, cols] = val[:32]
                we[1, half, cols] = val[32:]

    def send_piece(su, qu, h, target):
        remote(tpiece(su, qu, h), tpiece(su, qu, h), ts.at[0], tr.at[su * 4 + qu, h], target).start()

    def wait_piece(su, qu, h):
        remote(tpiece(su, qu, h), tpiece(su, qu, h), ts.at[0], tr.at[su * 4 + qu, h], other).wait_recv()

    def forward(line, early):
        su, qu = piece(line, v)

        @pl.when(jnp.logical_and(line != u, pick(EARLY, su) == early))
        def _():
            for h in range(2):
                wait_piece(su, qu, h)
                for d in (1, 3, 2):
                    send_piece(su, qu, h, dev(u, (v + d) % 4))

    for h in range(2):
        wait_piece(s0, q0, h)
        for d in (1, 3, 2):
            send_piece(s0, q0, h, dev((u + d) % 4, v))
    for early in (1, 0):

        @pl.when(pick(EARLY, s0) == early)
        def _():
            for h in range(2):
                for d in (1, 3, 2):
                    send_piece(s0, q0, h, dev(u, (v + d) % 4))

        for off in (0, 3, 1, 2):
            forward((u0 + off) % 4, early)

    def swap(slot):
        for b in range(2):
            x_ = (x0 + PLACE[slot][0]) % 4
            y_ = (y0 + 2 * PLACE[slot][1] + b) % 4
            q_ = 2 * b + k
            for h in range(2):

                @pl.when(y_ + k * (x_ - y_) != v)
                def _(q_=q_, h=h):
                    wait_piece(slot, q_, h)

                send_piece(slot, q_, h, other)

    def ready(slot):
        for b in range(2):
            for h in range(2):
                wait_piece(slot, 2 * b + 1 - k, h)

    def transposed(slot, s):
        cols = slice(s * QW, s * QW + QW)
        tt[cols, slot * TB : slot * TB + TB] = tv[slot, :, cols].T

    def b_copy(d, step, s, h):
        i = 4 * step + s
        return remote(sb.at[d, i, HALVES[h]], rb.at[d, i, HALVES[h]], bs.at[d], br.at[d, i, h], ring[d])

    def b_in(d, step, s, h):
        b_copy(d, step, s, h).wait_recv()
        return rb[d, 4 * step + s, HALVES[h], :].astype(F32)

    def b_out(d, step, s, h, val):
        sb[d, 4 * step + s, HALVES[h], :] = val.astype(BF16)
        b_copy(d, step, s, h).start()

    def partial_sum(slot, count, s):
        rows = tv[slot : slot + count].reshape(count * TB, DB)
        return jnp.dot(rows, wp[:, s * SW : s * SW + SW], preferred_element_type=F32)

    for slot in (7, 5, 6):
        swap(slot)
    ready(7)
    for s in range(NS):
        val = partial_sum(7, 1, s)
        for d in range(2):
            b_out(d, 0, s, d, val[HALVES[d]])
    ready(5)
    ready(6)

    def first(s):
        val = partial_sum(5, 2, s)
        for d in range(2):
            b_out(d, 1, s, 1 - d, val[d * TB + (1 - d) * HB : d * TB + (2 - d) * HB])
        return [val[d * TB + d * HB : d * TB + (1 + d) * HB] for d in range(2)]

    def second(s, rest):
        for d in range(2):
            b_out(d, 1, s, d, rest[d] + b_in(d, 0, s, d))

    rests = [first(0), first(1)]
    for s in range(NS):
        for slot in (7, 5, 6):
            transposed(slot, s)
    second(0, rests[0])
    rests.append(first(2))
    second(1, rests[1])
    rests.append(first(3))
    second(2, rests[2])
    second(3, rests[3])
    swap(3)
    swap(4)
    for step, slot in ((2, 3), (3, 1)):
        ready(slot)
        ready(slot + 1)
        for s in range(NS):
            if step == 2 and s == 1:
                for late in (1, 2, 0):
                    swap(late)
            val = partial_sum(slot, 2, s)
            for i in range(2):
                for d in range(2):
                    h = (1 - d + i) % 2
                    b_out(d, step, s, h, val[d * TB + h * HB : d * TB + h * HB + HB] + b_in(d, step - 1, s, h))
    ready(0)

    def d_copy(dst, src, s, h, d):
        cols = slice(s * SW, s * SW + SW)
        there, here = gv.at[dst, HALVES[h], cols], gv.at[src, HALVES[h], cols]
        return remote(here, there, dsm.at[d], dr.at[dst, s, h], ring[d])

    def d_wait(slot, s, h):
        d_copy(slot, slot, s, h, 0).wait_recv()

    for s in range(NS):
        own = partial_sum(0, 1, s)
        hcols = slice(s * 128, s * 128 + 128)
        for h in range(2):
            val = own[HALVES[h]]
            for d in range(2):
                val = val + b_in(d, 3, s, h)
            gate, up = val[:, :128], val[:, 128:]
            up_grad = ghv[HALVES[h], hcols].astype(F32)
            sig = 1.0 / (1.0 + jnp.exp(-gate))
            act = gate * sig
            gate_grad = up_grad * up * sig * (1.0 + gate * (1.0 - sig))
            gv[0, HALVES[h], s * SW : s * SW + 128] = gate_grad.astype(BF16)
            gv[0, HALVES[h], s * SW + 128 : s * SW + SW] = (up_grad * act).astype(BF16)
            d_copy(2, 0, s, h, 0).start()
            d_copy(1, 0, s, h, 1).start()
            hidden[HALVES[h], hcols] = (act * up).astype(BF16)
    store_h = pltpu.make_async_copy(hidden, hidden_out, osem.at[0])
    store_h.start()

    def of_group(one, two, g):
        return one.at[g // 4] if GROUPS[g][1] == 1 else two.at[g - 1]

    def core_dot(g, side):
        first, count = GROUPS[g]
        grads = gv[first : first + count].reshape(count * TB, DB)
        out = lax.dot_general(we[side], grads, (((1,), (1,)), ((), ())), preferred_element_type=F32)
        return out.reshape(16, 32, count * TB)

    def core_copy(g):
        return remote(of_group(ps1, ps2, g), of_group(cr1, cr2, g), ecs.at[g], ecr.at[g], other)

    def e1(g):
        of_group(ps1, ps2, g)[...] = core_dot(g, 1 - k).astype(BF16)
        core_copy(g).start()

    def own_dot(g):
        of_group(ow1, ow2, g)[...] = core_dot(g, k)

    def e2(g):
        core_copy(g).wait_recv()
        sums = of_group(sx1, sx2, g)
        sums[...] = (of_group(ow1, ow2, g)[...] + of_group(cr1, cr2, g)[...].astype(F32)).astype(BF16)
        for d in range(1, 16):
            chip = ((x + d // 4) % 4) * 4 + (y + d % 4) % 4
            remote(sums.at[chip], of_group(er1, er2, g).at[d - 1], exs.at[g], exr.at[g], near[d]).start()

    def plane_all(g):
        sums, got = of_group(sx1, sx2, g), of_group(er1, er2, g)
        return remote(sums.at[0:15], got, exs.at[g], exr.at[g], other)

    def e3(g):
        first, count = GROUPS[g]
        plane_all(g).wait_recv()
        val = of_group(sx1, sx2, g)[m].astype(F32)
        for d in range(15):
            val = val + of_group(er1, er2, g)[d].astype(F32)
        val = val.astype(BF16)
        for j in range(count):
            block = (z + NZ + OFFSET[first + j]) % NZ
            git[:, pl.ds(pl.multiple_of(block * TB, TB), TB)] = val[:, j * TB : j * TB + TB]

    for step in range(1, 4):
        for s in range(NS):
            for h in range(2):
                for d, slot in ((0, 2 * step), (1, 2 * step - 1)):
                    d_wait(slot, s, h)
                    if step < 3 or h == d:
                        d_copy(min(slot + 2, 7), slot, s, h, d).start()
            if s == 0:
                e1(step - 1)
            elif s == 1:
                own_dot(step - 1)
            elif s == 2:
                e2(step - 1)
            else:
                if step > 1:
                    e3(step - 2)
                for i in range(NS):
                    for slot in ((3, 4), (1, 2), (0,))[step - 1]:
                        transposed(slot, i)
    for s in range(NS):
        for h in range(2):
            d_wait(7, s, h)
        if s == 0:
            e1(3)
        elif s == 1:
            own_dot(3)
        elif s == 2:
            e2(3)
    e1(4)
    own_dot(4)
    e2(4)

    def store_rows(i):
        rows = slice(i * 256, i * 256 + 256)
        return [
            pltpu.make_async_copy(val.at[rows], out.at[rows], osem.at[2 + 2 * i + j])
            for j, (val, out) in enumerate(((og, og_out), (ou, ou_out)))
        ]

    def weight_rows(i):
        rows = slice(i * 256, i * 256 + 256)
        for s in range(NS):
            right = gv[:, :, s * SW : s * SW + SW].reshape(NZ * TB, SW)
            val = jnp.dot(tt[rows, :], right, preferred_element_type=F32)
            for b in range(4):
                row = i * 4 + b
                for which, out in enumerate((og, ou)):
                    cols = slice(s * SW + which * 128, s * SW + which * 128 + 128)
                    keep = mex[row, 0:1, cols] > 0.0
                    part = val[b * 64 : b * 64 + 64, which * 128 : which * 128 + 128]
                    out[row * 64 : row * 64 + 64, s * 128 : s * 128 + 128] = jnp.where(keep, part, 0.0).astype(BF16)
        for copy in store_rows(i):
            copy.start()

    for i in range(4):
        weight_rows(i)
    e3(2)
    e3(3)
    e3(4)
    store_i = pltpu.make_async_copy(git, git_out, osem.at[1])
    store_i.start()

    remote(tv, tv, ts.at[0], tr.at[0, 0], other).wait_send()
    for d in range(2):
        remote(sb.at[d, 0:14], sb.at[d, 0:14], bs.at[d], br.at[0, 0, 0], other).wait_send()
        remote(sb.at[d, 0:14], sb.at[d, 0:14], dsm.at[d], br.at[0, 0, 0], other).wait_send()
    for g in range(len(GROUPS)):
        core_copy(g).wait_send()
        plane_all(g).wait_send()
    store_h.wait()
    for i in range(4):
        for copy in store_rows(i):
            copy.wait()
    store_i.wait()


def finish(*refs):
    srcs, outs, held, sem = refs[:4], refs[4:8], refs[8:12], refs[12]
    parts = [(i, slice(j, j + 512)) for i in range(2, 4) for j in (0, 512)] + [(0, slice(0, TB)), (1, slice(0, 32))]
    loads = [pltpu.make_async_copy(srcs[i].at[r], held[i].at[r], sem.at[0, n]) for n, (i, r) in enumerate(parts)]
    stores = [pltpu.make_async_copy(held[i].at[r], outs[i].at[r], sem.at[1, n]) for n, (i, r) in enumerate(parts)]
    for load in loads:
        load.start()
    for load, store in zip(loads, stores):
        load.wait()
        store.start()
    for store in stores:
        store.wait()


def shards(tokens, gate_weight, up_weight, gate_mask, up_mask, grad_hidden):
    hbm = pl.BlockSpec(memory_space=pl.ANY)
    dma = pltpu.SemaphoreType.DMA
    ng = len(GROUPS)
    shapes = (
        jax.ShapeDtypeStruct((TB, 512), BF16),
        jax.ShapeDtypeStruct((32, NZ * TB), BF16),
        jax.ShapeDtypeStruct((DB, 512), BF16),
        jax.ShapeDtypeStruct((DB, 512), BF16),
    )
    results = pl.pallas_call(
        kernel,
        out_shape=shapes,
        in_specs=[hbm] * 6,
        out_specs=(hbm,) * 4,
        scratch_shapes=[
            pltpu.VMEM((8, 16), jnp.int32),
            pltpu.VMEM((8, 16), jnp.int32),
            pltpu.VMEM((DB, 512), BF16),
            pltpu.VMEM((DB, 512), BF16),
            pltpu.VMEM((TB, 512), BF16),
            pltpu.VMEM((TB, 512), BF16),
            pltpu.VMEM((32, NZ * TB), BF16),
            pltpu.VMEM((DB, 512), BF16),
            pltpu.VMEM((DB, 512), BF16),
            pltpu.VMEM((DB, DB), BF16),
            pltpu.VMEM((2, 512, DB), BF16),
            pltpu.VMEM((16, 8, DB), F32),
            pltpu.VMEM((NZ, TB, DB), BF16),
            pltpu.VMEM((DB, NZ * TB), BF16),
            pltpu.VMEM((2, 16, TB, SW), BF16),
            pltpu.VMEM((2, 16, TB, SW), BF16),
            pltpu.VMEM((NZ, TB, DB), BF16),
            pltpu.VMEM((2, 16, 32, TB), BF16),
            pltpu.VMEM((3, 16, 32, 2 * TB), BF16),
            pltpu.VMEM((2, 16, 32, TB), BF16),
            pltpu.VMEM((3, 16, 32, 2 * TB), BF16),
            pltpu.VMEM((2, 16, 32, TB), F32),
            pltpu.VMEM((3, 16, 32, 2 * TB), F32),
            pltpu.VMEM((2, 16, 32, TB), BF16),
            pltpu.VMEM((3, 16, 32, 2 * TB), BF16),
            pltpu.VMEM((2, 15, 32, TB), BF16),
            pltpu.VMEM((3, 15, 32, 2 * TB), BF16),
            dma((5,)),
            dma((10,)),
            dma((1,)),
            dma((32, 2)),
            dma((2,)),
            dma((2, 16, 2)),
            dma((2,)),
            dma((NZ, NS, 2)),
            dma((ng,)),
            dma((ng,)),
            dma((ng,)),
            dma((ng,)),
        ],
        compiler_params=pltpu.CompilerParams(
            collective_id=0, has_side_effects=True, vmem_limit_bytes=56 * 1024 * 1024
        ),
    )(tokens, gate_weight, up_weight, gate_mask.T, up_mask.T, grad_hidden)
    hidden, git, og, ou = pl.pallas_call(
        finish,
        out_shape=shapes,
        in_specs=[hbm] * 4,
        out_specs=(hbm,) * 4,
        scratch_shapes=[pltpu.VMEM(shape.shape, BF16) for shape in shapes] + [dma((2, 6))],
        compiler_params=pltpu.CompilerParams(vmem_limit_bytes=56 * 1024 * 1024),
    )(*results)
    return hidden, git.T, og, ou


def solution(mesh):
    return jax.shard_map(
        shards,
        mesh=mesh,
        in_specs=(P("row", "col"),) * 6,
        out_specs=(P("row", "col"), P(None, ("row", "col")), P("row", "col"), P("row", "col")),
        check_vma=False,
    )
```

```python
import jax
import jax.numpy as jnp
from jax import lax
from jax.experimental import pallas as pl
from jax.experimental.pallas import tpu as pltpu
from jax.sharding import PartitionSpec as P

MESH = pl.DeviceIdType.MESH
BF16 = jnp.bfloat16
F32 = jnp.float32

NZ = 8
NS = 4
TB = 128
DB = 1024
SW = 256
QW = 256
HB = 64
HALVES = (slice(0, HB), slice(HB, TB))
OFFSET = (0, 1, -1, 2, -2, 3, -3, 4)
GROUPS = ((0, 1), (1, 2), (3, 2), (5, 2), (7, 1))
PLACE = ((2, 0), (1, 1), (2, 1), (0, 0), (3, 1), (3, 0), (0, 1), (1, 0))
SLOT_AT = tuple(PLACE.index((i % 4, i // 4)) for i in range(8))
REL = tuple(o % NZ for o in OFFSET)
EARLY = (0, 0, 0, 0, 0, 1, 1, 1)
SLOT_OF = tuple(REL.index(r) for r in range(NZ))


FAR_FIRST = sorted(range(1, 16), key=lambda d: -(min(d // 4, 4 - d // 4) + min(d % 4, 4 - d % 4)))


def pick(table, i):
    return sum(t * (1 - ((i - j) * (i - j) + 63) // 64) for j, t in enumerate(table))


def remote(src, dst, send, recv, device):
    return pltpu.make_async_remote_copy(
        src_ref=src, dst_ref=dst, send_sem=send, recv_sem=recv, device_id=device, device_id_type=MESH
    )


def kernel(
    tokens, wg, wu, mg, mu, gh,
    hidden_out, git_out, og_out, ou_out,
    mgv, muv, wgv, wuv, ghv, hidden, git, og, ou, wp, we, mex, tv, tt, sb, rb, gv,
    ps1, ps2, cr1, cr2, ow1, ow2, sx1, sx2, er1, er2,
    lsem, osem, ts, tr, bs, br, dsm, dr, ecs, ecr, exs, exr,
):
    z = lax.axis_index("row")
    c = lax.axis_index("col")
    m = c // 2
    k = c % 2
    x, y = m // 4, m % 4
    u = x + k * (y - x)
    v = y + k * (x - y)
    x0, y0 = z // 2, 2 * (z % 2)
    u0 = x0 + k * (y0 - x0)

    def dev(u_, v_):
        x_ = u_ + k * (v_ - u_)
        y_ = v_ + k * (u_ - v_)
        return (z, (x_ * 4 + y_) * 2 + k)

    def tpiece(slot, q_, h):
        return tv.at[slot, HALVES[h], pl.ds(pl.multiple_of(q_ * QW, QW), QW)]

    def piece(u_, v_):
        dx = (u_ + k * (v_ - u_) + 4 - x0) % 4
        dy = (v_ + k * (u_ - v_) + 4 - y0) % 4
        return pick(SLOT_AT, dx + 4 * (dy // 2)), 2 * (dy % 2) + k

    upd = ((z + 1) % NZ, c)
    down = ((z + NZ - 1) % NZ, c)
    ring = (upd, down)
    other = (z, c + 1 - 2 * k)

    plane = c // 4
    slot_there = pick(SLOT_OF, (z + NZ - plane) % NZ)
    to_x = (plane // 2 + pick([p[0] for p in PLACE], slot_there)) % 4
    to_y = (2 * (plane % 2) + 2 * pick([p[1] for p in PLACE], slot_there) + m % 2) % 4
    to = (plane, (to_x * 4 + to_y) * 2 + k)
    s0, q0 = piece(u, v)
    frm = ((z + pick(REL, s0)) % NZ, 4 * z + q0)

    load_mg = pltpu.make_async_copy(mg, mgv, lsem.at[3])
    load_mu = pltpu.make_async_copy(mu, muv, lsem.at[4])
    load_mg.start()
    load_mu.start()
    load_g = pltpu.make_async_copy(wg, wgv, lsem.at[0])
    load_u = pltpu.make_async_copy(wu, wuv, lsem.at[1])
    load_h = pltpu.make_async_copy(gh, ghv, lsem.at[2])
    load_g.start()
    load_u.start()
    load_h.start()

    barrier = pltpu.get_barrier_semaphore()
    near = [(z, (((x + d // 4) % 4) * 4 + (y + d % 4) % 4) * 2 + k) for d in range(16)]
    for target in near[1:] + [other, upd, down, frm]:
        pl.semaphore_signal(barrier, inc=1, device_id=target, device_id_type=MESH)
    pl.semaphore_wait(barrier, 19)

    for h in range(2):
        remote(
            tokens.at[HALVES[h]], tpiece(slot_there, c % 4, h), ts.at[0], tr.at[slot_there * 4 + c % 4, h], to
        ).start()

    lane = lax.broadcasted_iota(jnp.int32, (16, 128), 1) // 64
    load_mg.wait()
    load_mu.wait()
    for which, mask in enumerate((mgv, muv)):
        kept = jnp.where(mask[...] > 0, 1.0, 0.0).astype(F32).T
        for s in range(NS):
            kept_wide = jnp.where(lane == 0, kept[:, 2 * s : 2 * s + 1], kept[:, 2 * s + 1 : 2 * s + 2])
            for i in range(16):
                mex[i, :, s * SW + which * 128 : s * SW + which * 128 + 128] = jnp.broadcast_to(
                    kept_wide[i : i + 1], (8, 128)
                )
    load_g.wait()
    load_u.wait()
    load_h.wait()

    @pl.loop(0, 16)
    def _(i):
        rows = pl.ds(pl.multiple_of(i * 64, 64), 64)
        half = pl.ds(pl.multiple_of(i * 32, 32), 32)
        for s in range(NS):
            for which, raw in enumerate((wgv, wuv)):
                cols = slice(s * SW + which * 128, s * SW + which * 128 + 128)
                val = raw[rows, s * 128 : s * 128 + 128].astype(F32).reshape(8, 8, 128)
                val = (val * mex[i, :, cols]).reshape(64, 128).astype(BF16)
                wp[rows, cols] = val
                we[0, half, cols] = val[:32]
                we[1, half, cols] = val[32:]

    def send_piece(su, qu, h, target):
        remote(tpiece(su, qu, h), tpiece(su, qu, h), ts.at[0], tr.at[su * 4 + qu, h], target).start()

    def wait_piece(su, qu, h):
        remote(tpiece(su, qu, h), tpiece(su, qu, h), ts.at[0], tr.at[su * 4 + qu, h], other).wait_recv()

    def forward(line, early):
        su, qu = piece(line, v)

        @pl.when(jnp.logical_and(line != u, pick(EARLY, su) == early))
        def _():
            for h in range(2):
                wait_piece(su, qu, h)
                for d in (2, 1, 3):
                    send_piece(su, qu, h, dev(u, (v + d) % 4))

    for h in range(2):
        wait_piece(s0, q0, h)
        for d in (2, 1, 3):
            send_piece(s0, q0, h, dev((u + d) % 4, v))
    for early in (1, 0):

        @pl.when(pick(EARLY, s0) == early)
        def _():
            for h in range(2):
                for d in (2, 1, 3):
                    send_piece(s0, q0, h, dev(u, (v + d) % 4))

        for off in (0, 3, 1, 2):
            forward((u0 + off) % 4, early)

    def swap(slot):
        for b in range(2):
            x_ = (x0 + PLACE[slot][0]) % 4
            y_ = (y0 + 2 * PLACE[slot][1] + b) % 4
            q_ = 2 * b + k
            for h in range(2):

                @pl.when(y_ + k * (x_ - y_) != v)
                def _(q_=q_, h=h):
                    wait_piece(slot, q_, h)

                send_piece(slot, q_, h, other)

    def ready(slot):
        for b in range(2):
            for h in range(2):
                wait_piece(slot, 2 * b + 1 - k, h)

    def transposed(slot, s):
        cols = slice(s * QW, s * QW + QW)
        tt[cols, slot * TB : slot * TB + TB] = tv[slot, :, cols].T

    def b_copy(d, step, s, h):
        i = 4 * step + s
        return remote(sb.at[d, i, HALVES[h]], rb.at[d, i, HALVES[h]], bs.at[d], br.at[d, i, h], ring[d])

    def b_in(d, step, s, h):
        b_copy(d, step, s, h).wait_recv()
        return rb[d, 4 * step + s, HALVES[h], :].astype(F32)

    def b_out(d, step, s, h, val):
        sb[d, 4 * step + s, HALVES[h], :] = val.astype(BF16)
        b_copy(d, step, s, h).start()

    def partial_sum(slot, count, s):
        rows = tv[slot : slot + count].reshape(count * TB, DB)
        return jnp.dot(rows, wp[:, s * SW : s * SW + SW], preferred_element_type=F32)

    for slot in (7, 5, 6):
        swap(slot)
    ready(7)
    for s in range(NS):
        val = partial_sum(7, 1, s)
        for d in range(2):
            b_out(d, 0, s, d, val[HALVES[d]])
    ready(5)
    ready(6)

    def first(s):
        val = partial_sum(5, 2, s)
        for d in range(2):
            b_out(d, 1, s, 1 - d, val[d * TB + (1 - d) * HB : d * TB + (2 - d) * HB])
        return [val[d * TB + d * HB : d * TB + (1 + d) * HB] for d in range(2)]

    def second(s, rest):
        for d in range(2):
            b_out(d, 1, s, d, rest[d] + b_in(d, 0, s, d))

    rests = [first(0), first(1)]
    for s in range(NS):
        for slot in (7, 5, 6):
            transposed(slot, s)
    second(0, rests[0])
    rests.append(first(2))
    second(1, rests[1])
    rests.append(first(3))
    second(2, rests[2])
    second(3, rests[3])
    swap(3)
    swap(4)
    for step, slot in ((2, 3), (3, 1)):
        ready(slot)
        ready(slot + 1)
        for s in range(NS):
            if step == 2 and s == 1:
                for late in (1, 2, 0):
                    swap(late)
            val = partial_sum(slot, 2, s)
            for i in range(2):
                for d in range(2):
                    h = (1 - d + i) % 2
                    b_out(d, step, s, h, val[d * TB + h * HB : d * TB + h * HB + HB] + b_in(d, step - 1, s, h))
    ready(0)

    def d_copy(dst, src, s, h, d):
        cols = slice(s * SW, s * SW + SW)
        there, here = gv.at[dst, HALVES[h], cols], gv.at[src, HALVES[h], cols]
        return remote(here, there, dsm.at[d], dr.at[dst, s, h], ring[d])

    def d_wait(slot, s, h):
        d_copy(slot, slot, s, h, 0).wait_recv()

    for s in range(NS):
        own = partial_sum(0, 1, s)
        hcols = slice(s * 128, s * 128 + 128)
        for h in range(2):
            val = own[HALVES[h]]
            for d in range(2):
                val = val + b_in(d, 3, s, h)
            gate, up = val[:, :128], val[:, 128:]
            up_grad = ghv[HALVES[h], hcols].astype(F32)
            sig = 1.0 / (1.0 + jnp.exp(-gate))
            act = gate * sig
            gate_grad = up_grad * up * sig * (1.0 + gate * (1.0 - sig))
            gv[0, HALVES[h], s * SW : s * SW + 128] = gate_grad.astype(BF16)
            gv[0, HALVES[h], s * SW + 128 : s * SW + SW] = (up_grad * act).astype(BF16)
            d_copy(2, 0, s, h, 0).start()
            d_copy(1, 0, s, h, 1).start()
            hidden[HALVES[h], hcols] = (act * up).astype(BF16)
    store_h = pltpu.make_async_copy(hidden, hidden_out, osem.at[0])
    store_h.start()

    def of_group(one, two, g):
        return one.at[g // 4] if GROUPS[g][1] == 1 else two.at[g - 1]

    def core_dot(g, side):
        first, count = GROUPS[g]
        grads = gv[first : first + count].reshape(count * TB, DB)
        out = lax.dot_general(we[side], grads, (((1,), (1,)), ((), ())), preferred_element_type=F32)
        return out.reshape(16, 32, count * TB)

    def core_copy(g):
        return remote(of_group(ps1, ps2, g), of_group(cr1, cr2, g), ecs.at[g], ecr.at[g], other)

    def e1(g):
        of_group(ps1, ps2, g)[...] = core_dot(g, 1 - k).astype(BF16)
        core_copy(g).start()

    def own_dot(g):
        of_group(ow1, ow2, g)[...] = core_dot(g, k)

    def e2(g):
        core_copy(g).wait_recv()
        sums = of_group(sx1, sx2, g)
        sums[...] = (of_group(ow1, ow2, g)[...] + of_group(cr1, cr2, g)[...].astype(F32)).astype(BF16)
        for d in FAR_FIRST:
            chip = ((x + d // 4) % 4) * 4 + (y + d % 4) % 4
            remote(sums.at[chip], of_group(er1, er2, g).at[d - 1], exs.at[g], exr.at[g], near[d]).start()

    def plane_all(g):
        sums, got = of_group(sx1, sx2, g), of_group(er1, er2, g)
        return remote(sums.at[0:15], got, exs.at[g], exr.at[g], other)

    def e3(g):
        first, count = GROUPS[g]
        plane_all(g).wait_recv()
        val = of_group(sx1, sx2, g)[m].astype(F32)
        for d in range(15):
            val = val + of_group(er1, er2, g)[d].astype(F32)
        val = val.astype(BF16)
        for j in range(count):
            block = (z + NZ + OFFSET[first + j]) % NZ
            git[:, pl.ds(pl.multiple_of(block * TB, TB), TB)] = val[:, j * TB : j * TB + TB]

    for step in range(1, 4):
        for s in range(NS):
            for h in range(2):
                for d, slot in ((0, 2 * step), (1, 2 * step - 1)):
                    d_wait(slot, s, h)
                    if step < 3 or h == d:
                        d_copy(min(slot + 2, 7), slot, s, h, d).start()
            if s == 0:
                e1(step - 1)
            elif s == 1:
                own_dot(step - 1)
            elif s == 2:
                e2(step - 1)
            else:
                if step > 1:
                    e3(step - 2)
                for i in range(NS):
                    for slot in ((3, 4), (1, 2), (0,))[step - 1]:
                        transposed(slot, i)
    for s in range(NS):
        for h in range(2):
            d_wait(7, s, h)
        if s == 0:
            e1(3)
        elif s == 1:
            own_dot(3)
        elif s == 2:
            e2(3)
    e1(4)
    own_dot(4)
    e2(4)

    def store_rows(i):
        rows = slice(i * 256, i * 256 + 256)
        return [
            pltpu.make_async_copy(val.at[rows], out.at[rows], osem.at[2 + 2 * i + j])
            for j, (val, out) in enumerate(((og, og_out), (ou, ou_out)))
        ]

    def weight_rows(i):
        rows = slice(i * 256, i * 256 + 256)
        for s in range(NS):
            right = gv[:, :, s * SW : s * SW + SW].reshape(NZ * TB, SW)
            val = jnp.dot(tt[rows, :], right, preferred_element_type=F32)
            for b in range(4):
                row = i * 4 + b
                for which, out in enumerate((og, ou)):
                    cols = slice(s * SW + which * 128, s * SW + which * 128 + 128)
                    keep = mex[row, 0:1, cols] > 0.0
                    part = val[b * 64 : b * 64 + 64, which * 128 : which * 128 + 128]
                    out[row * 64 : row * 64 + 64, s * 128 : s * 128 + 128] = jnp.where(keep, part, 0.0).astype(BF16)
        for copy in store_rows(i):
            copy.start()

    for i in range(4):
        weight_rows(i)
    e3(2)
    e3(3)
    e3(4)
    store_i = pltpu.make_async_copy(git, git_out, osem.at[1])
    store_i.start()

    remote(tv, tv, ts.at[0], tr.at[0, 0], other).wait_send()
    for d in range(2):
        remote(sb.at[d, 0:14], sb.at[d, 0:14], bs.at[d], br.at[0, 0, 0], other).wait_send()
        remote(sb.at[d, 0:14], sb.at[d, 0:14], dsm.at[d], br.at[0, 0, 0], other).wait_send()
    for g in range(len(GROUPS)):
        core_copy(g).wait_send()
        plane_all(g).wait_send()
    store_h.wait()
    for i in range(4):
        for copy in store_rows(i):
            copy.wait()
    store_i.wait()


def finish(*refs):
    srcs, outs, held, sem = refs[:4], refs[4:8], refs[8:12], refs[12]
    parts = [(i, slice(j, j + 512)) for i in range(2, 4) for j in (0, 512)] + [(0, slice(0, TB)), (1, slice(0, 32))]
    loads = [pltpu.make_async_copy(srcs[i].at[r], held[i].at[r], sem.at[0, n]) for n, (i, r) in enumerate(parts)]
    stores = [pltpu.make_async_copy(held[i].at[r], outs[i].at[r], sem.at[1, n]) for n, (i, r) in enumerate(parts)]
    for load in loads:
        load.start()
    for load, store in zip(loads, stores):
        load.wait()
        store.start()
    for store in stores:
        store.wait()


def shards(tokens, gate_weight, up_weight, gate_mask, up_mask, grad_hidden):
    hbm = pl.BlockSpec(memory_space=pl.ANY)
    dma = pltpu.SemaphoreType.DMA
    ng = len(GROUPS)
    shapes = (
        jax.ShapeDtypeStruct((TB, 512), BF16),
        jax.ShapeDtypeStruct((32, NZ * TB), BF16),
        jax.ShapeDtypeStruct((DB, 512), BF16),
        jax.ShapeDtypeStruct((DB, 512), BF16),
    )
    results = pl.pallas_call(
        kernel,
        out_shape=shapes,
        in_specs=[hbm] * 6,
        out_specs=(hbm,) * 4,
        scratch_shapes=[
            pltpu.VMEM((8, 16), jnp.int32),
            pltpu.VMEM((8, 16), jnp.int32),
            pltpu.VMEM((DB, 512), BF16),
            pltpu.VMEM((DB, 512), BF16),
            pltpu.VMEM((TB, 512), BF16),
            pltpu.VMEM((TB, 512), BF16),
            pltpu.VMEM((32, NZ * TB), BF16),
            pltpu.VMEM((DB, 512), BF16),
            pltpu.VMEM((DB, 512), BF16),
            pltpu.VMEM((DB, DB), BF16),
            pltpu.VMEM((2, 512, DB), BF16),
            pltpu.VMEM((16, 8, DB), F32),
            pltpu.VMEM((NZ, TB, DB), BF16),
            pltpu.VMEM((DB, NZ * TB), BF16),
            pltpu.VMEM((2, 16, TB, SW), BF16),
            pltpu.VMEM((2, 16, TB, SW), BF16),
            pltpu.VMEM((NZ, TB, DB), BF16),
            pltpu.VMEM((2, 16, 32, TB), BF16),
            pltpu.VMEM((3, 16, 32, 2 * TB), BF16),
            pltpu.VMEM((2, 16, 32, TB), BF16),
            pltpu.VMEM((3, 16, 32, 2 * TB), BF16),
            pltpu.VMEM((2, 16, 32, TB), F32),
            pltpu.VMEM((3, 16, 32, 2 * TB), F32),
            pltpu.VMEM((2, 16, 32, TB), BF16),
            pltpu.VMEM((3, 16, 32, 2 * TB), BF16),
            pltpu.VMEM((2, 15, 32, TB), BF16),
            pltpu.VMEM((3, 15, 32, 2 * TB), BF16),
            dma((5,)),
            dma((10,)),
            dma((1,)),
            dma((32, 2)),
            dma((2,)),
            dma((2, 16, 2)),
            dma((2,)),
            dma((NZ, NS, 2)),
            dma((ng,)),
            dma((ng,)),
            dma((ng,)),
            dma((ng,)),
        ],
        compiler_params=pltpu.CompilerParams(
            collective_id=0, has_side_effects=True, vmem_limit_bytes=56 * 1024 * 1024
        ),
    )(tokens, gate_weight, up_weight, gate_mask.T, up_mask.T, grad_hidden)
    hidden, git, og, ou = pl.pallas_call(
        finish,
        out_shape=shapes,
        in_specs=[hbm] * 4,
        out_specs=(hbm,) * 4,
        scratch_shapes=[pltpu.VMEM(shape.shape, BF16) for shape in shapes] + [dma((2, 6))],
        compiler_params=pltpu.CompilerParams(vmem_limit_bytes=56 * 1024 * 1024),
    )(*results)
    return hidden, git.T, og, ou


def solution(mesh):
    return jax.shard_map(
        shards,
        mesh=mesh,
        in_specs=(P("row", "col"),) * 6,
        out_specs=(P("row", "col"), P(None, ("row", "col")), P("row", "col"), P("row", "col")),
        check_vma=False,
    )
```
